1024 devices in a mesh: ep: 16 (over x, y_lo, core), dp: 64 (over y_hi, z).
Axes of the slice: x: 4, y: 4 (y_hi: 2, y_lo: 2; y = y_hi * 2 + y_lo), z: 32, core: 2. Of those that a mesh axis runs over, the one named last changes fastest.
Arguments:
- tokens: bfloat16 [2048, 3584], P('dp'), may hold values from -6 to 6
- gate_scores: float32 [2048, 8], P('dp'), may hold values from 0.05 to 1
- routes: int32 [2048, 8], P('dp'), may hold values from 0 to 127, all different within a row; in each aligned block of 32 rows (0 to 31, 32 to 63, ...) at most 4 rows name the same one
- balanced: int32 [64, 16], P(None, 'ep'), may hold values from 0 to 1, as said below
- gate_up: bfloat16 [64, 16, 3584, 256], P('dp', 'ep'), may hold values from -0.09375 to 0.09375
- down_proj: bfloat16 [64, 16, 128, 3584], P('dp', 'ep'), may hold values from -0.1875 to 0.1875
Outputs:
- mixed: float32 [2048, 3584], P('dp', 'ep')
The draws below stay inside these ranges and needn't reach their ends.
Inputs may be any that keep to these rules, and one draw needn't show every extreme that they name: `routes`: among the tokens of one dp index no expert is named more than 4 times, a bound that some block reaches. balanced[d, i] equals balanced[d + 32, i] for d < 32.
All inputs are finite; a program needn't handle non-finite values.
Results may differ from the reference program's by a relative error of at most 0.007.
Values may be sent and summed in bfloat16 or wider, within the bound.
No kernel may reach another device: no remote copies, remote signals or barrier semaphores. Data moves between devices by JAX's collectives and lax.ppermute only.
A program may use at most 64 MiB of HBM per device.

```python
import math
import jax
import jax.numpy as jnp
import numpy as np
from jax import lax

D = 3584
F = 1024
TOP = 8
TOK_G = 32
SPLIT = 8
HT = 128
EXPERTS = 128
CAP = 4
TOKENS = 2048
N_EP = 16
N_DP = 64


def draw_balanced(key, part):
    key = jax.random.fold_in(key, 7)
    upper = jax.random.randint(key, (N_DP // 2, N_EP), 0, 2, dtype=jnp.int32)
    return jnp.concatenate([upper, upper], axis=0)


def steps_of(own_key, extent, pieces, low, largest):
    def one(axis_at, shards_of):
        heights = jax.random.uniform(jax.random.fold_in(jax.random.fold_in(own_key, 6), axis_at), (shards_of,), jnp.float32, low / len(pieces), largest / len(pieces))
        return jnp.repeat(jnp.exp(heights), extent[axis_at] // shards_of).reshape((-1,) + (1,) * (len(extent) - axis_at - 1))

    factor_of = one(*pieces[0])
    for cut in pieces[1:]:
        factor_of = factor_of * one(*cut)
    return factor_of


def routed_block(key, own, number, rows, count, top, limit, slope):
    sequence = jax.random.permutation(key, count)
    heavy_load, usual = shares(count, rows * top, limit, slope, True), shares(count, rows * top, limit, slope, False)
    places = jnp.arange(count)

    def named(tallies, turn):
        used = int((tallies > 0).sum())
        fixed = max(1, used // 4)
        shifted = fixed + (places - fixed + turn * (used - fixed)) % max(1, count - fixed)
        return jnp.zeros((count,), jnp.int32).at[sequence[jnp.where(places < fixed, places, shifted)]].set(jnp.asarray(tallies, jnp.int32))

    tallies = jnp.where(number % 4 == 0, named(heavy_load, number // 4), named(usual, number - number // 4 - 1))
    mixed = jax.random.permutation(jax.random.fold_in(own, 3), count)
    donor, taker = mixed[0:count // 2 * 2:2], mixed[1:count // 2 * 2:2]
    room = jnp.minimum(tallies[donor] - 1, limit - tallies[taker]) // 2
    room = jnp.where((donor == sequence[0]) | (taker == sequence[0]) | (tallies[taker] == 0), 0, jnp.maximum(room, 0))
    shifted = jax.random.randint(jax.random.fold_in(own, 4), (count // 2,), 0, 1 << 20) % (room + 1)
    tallies = tallies.at[donor].add(-shifted).at[taker].add(shifted)
    members = jnp.searchsorted(jnp.cumsum(tallies), jnp.arange(rows * top), side="right").astype(jnp.int32)
    listing = members.reshape(top, rows).T
    listing = listing[jax.random.permutation(jax.random.fold_in(own, 1), rows)]
    turn = jax.random.randint(jax.random.fold_in(own, 2), (rows, 1), 0, top)
    return jnp.take_along_axis(listing, (jnp.arange(top)[None, :] + turn) % top, axis=1)


def shares(number_of, total, bound, lean, full):
    portions = [(1 << 20) // math.isqrt(rank ** lean) + 1 for rank in range(1, number_of + 1)]
    largest = bound if full else min(bound, max(-(-total // number_of), total * portions[0] // sum(portions)))
    least = 1 if total - largest >= number_of - 1 else 0
    holding, rest = [largest] + [least] * (number_of - 1), total - largest - least * (number_of - 1)
    while rest > 0:
        movable = [i for i in range(1, number_of) if holding[i] < largest] or [i for i in range(1, number_of) if holding[i] < bound]
        pool, remaining = sum([portions[i] for i in movable]), rest
        for i in movable:
            addition = min(bound - holding[i], max(1, remaining * portions[i] // pool), rest)
            holding[i] = holding[i] + addition
            rest = rest - addition
    return np.array(holding)


def scatter_about(rng, shape, width, most, cuts=(), kind=jnp.bfloat16):
    loudness = steps_of(rng, shape, cuts, -0.22, 0.18) if cuts else 1.0
    array = jax.random.normal(rng, shape, jnp.float32) * width * loudness
    return jnp.minimum(jnp.maximum(array, -most), most).astype(kind)


def setup_inputs(seed: int = 0) -> dict:
    seeds = jax.random.split(jax.random.key(seed), 7)
    tokens = scatter_about(seeds[0], (TOKENS, D), 1.0, 6.0, ((0, 64),))
    gate_scores = jnp.clip(jnp.exp(math.log(1.0) - 2.9957323 * jax.random.uniform(seeds[1], (TOKENS, TOP), jnp.float32) ** steps_of(seeds[1], (TOKENS, TOP), ((0, 64),), -0.2, 0.2)), 0.05, 1.0)
    routes_keys = jax.random.split(jax.random.fold_in(seeds[2], 1), TOKENS // TOK_G)
    routes_turns = jax.random.permutation(jax.random.fold_in(seeds[2], 3), TOKENS // TOK_G)
    routes = jax.vmap(lambda own, number: routed_block(jax.random.fold_in(seeds[2], 2), own, number, TOK_G, EXPERTS, TOP, CAP, 2))(routes_keys, routes_turns).reshape((TOKENS, TOP))
    balanced = draw_balanced(jax.random.fold_in(seeds[6], 71), 0)
    gate_up = scatter_about(seeds[4], (N_DP, N_EP, D, 2 * HT), D ** -0.5, 0.09375, ((0, 64), (1, 16)))
    down_proj = scatter_about(seeds[5], (N_DP, N_EP, HT, D), F ** -0.5, 0.1875, ((0, 64), (1, 16)))
    return {"tokens": tokens, "gate_scores": gate_scores, "routes": routes, "balanced": balanced, "gate_up": gate_up, "down_proj": down_proj}


ROUTE_SCALE = 2.5


def slot_weights(gate_up, down_proj, balanced):
    half_way = N_DP // 2
    flag = (balanced == 1)[:, :, None, None]
    moved_up = jnp.where(flag, jnp.roll(gate_up, half_way, axis=0), gate_up)
    moved_down = jnp.where(flag, jnp.roll(down_proj, half_way, axis=0), down_proj)
    return moved_up.reshape(EXPERTS, SPLIT, D, 2 * HT), moved_down.reshape(EXPERTS, SPLIT, HT, D)


def reference(tokens, gate_scores, routes, balanced, gate_up, down_proj):
    weights_up, weights_down = slot_weights(gate_up, down_proj, balanced)
    scaled = gate_scores / jnp.sum(gate_scores, axis=1, keepdims=True) * ROUTE_SCALE
    rows_most = N_DP * CAP

    def one_expert(total, expert):
        chosen = routes == expert
        weight = jnp.sum(jnp.where(chosen, scaled, 0.0), axis=1)
        present = jnp.any(chosen, axis=1)
        count = jnp.sum(present.astype(jnp.int32))
        picked = jnp.nonzero(present, size=rows_most, fill_value=0)[0].astype(jnp.int32)
        valid = (jnp.arange(rows_most, dtype=jnp.int32) < count).astype(jnp.float32)
        rows = tokens[picked].astype(jnp.float32)
        expert_up = lax.dynamic_index_in_dim(weights_up, expert, 0, keepdims=False).astype(jnp.float32)
        expert_down = lax.dynamic_index_in_dim(weights_down, expert, 0, keepdims=False).astype(jnp.float32)
        projected = jnp.einsum('rd,sdh->rsh', rows, expert_up)
        hidden = (jax.nn.silu(projected[..., :HT]) * projected[..., HT:]).astype(jnp.bfloat16)
        partial_value = jnp.einsum('rsh,shd->rsd', hidden.astype(jnp.float32), expert_down).astype(jnp.bfloat16)
        term = jnp.sum(partial_value.astype(jnp.float32), axis=1) * (weight[picked] * valid)[:, None]
        return total.at[picked].add(term), None

    start = jnp.zeros((TOKENS, D), jnp.float32)
    total, unused = lax.scan(one_expert, start, jnp.arange(EXPERTS, dtype=jnp.int32))
    return total
```

```python
import jax
import jax.numpy as jnp
from jax import lax
from jax.experimental import pallas as pl
from jax.experimental.pallas import tpu as pltpu
from jax.sharding import Mesh, PartitionSpec as P

ROUTE_SCALE = 2.5
AXES = ("xh", "e", "yh", "z")
BF16, F32, I32 = jnp.bfloat16, jnp.float32, jnp.int32
SMEM = pl.BlockSpec(memory_space=pltpu.SMEM)
VMEM = pl.BlockSpec(memory_space=pltpu.VMEM)
PARAMS = pltpu.CompilerParams(vmem_limit_bytes=40 * 2**20)


def matmul(a, b, dims=((1,), (0,))):
    return lax.dot_general(a, b, (dims, ((), ())), preferred_element_type=F32)


def dispatch_kernel(lines, capacity, xh_ref, routes_ref, scores_ref, mine_ref, out_ref, weight_ref):
    tok_rows, top_count = routes_ref.shape
    rows = lines * 2 * capacity
    row = lax.broadcasted_iota(I32, (tok_rows, rows), 1)
    place = row % capacity
    half = row // capacity % 2
    line = row // (2 * capacity)
    expert_at = (half * lines + line) * 2 + xh_ref[0]
    routes = routes_ref[...]
    scores = scores_ref[...]
    scaled = scores / jnp.sum(scores, axis=1, keepdims=True) * ROUTE_SCALE
    weight = jnp.zeros((tok_rows, rows), F32)
    member = jnp.zeros((tok_rows, rows), F32)
    for k in range(top_count):
        match = routes[:, k : k + 1] == expert_at
        member = jnp.where(match, 1.0, member)
        weight = jnp.where(match, scaled[:, k : k + 1], weight)
    before = (
        lax.broadcasted_iota(I32, (tok_rows, tok_rows), 0)
        > lax.broadcasted_iota(I32, (tok_rows, tok_rows), 1)
    ).astype(F32)
    rank = matmul(before.astype(BF16), member.astype(BF16))
    chosen = jnp.where(rank == place.astype(F32), member, 0.0)
    weight = weight * chosen
    high = weight.astype(BF16)
    weight_ref[:tok_rows, :] = high
    weight_ref[tok_rows:, :] = (weight - high.astype(F32)).astype(BF16)
    selector = chosen.astype(BF16)
    for u in range(2):
        out_ref[u] = matmul(selector, mine_ref[u], ((0,), (0,))).astype(BF16)


def spread_kernel(capacity, wants_ref, arrived_ref, out_ref):
    total = arrived_ref.shape[0]
    rows = total // 2
    arrived = arrived_ref[...]
    source = lax.broadcasted_iota(I32, (total, rows), 0)
    row = lax.broadcasted_iota(I32, (total, rows), 1)
    wanted = row // capacity * (2 * capacity) + row % capacity
    picks = []
    for half in range(2):
        pick = (source == wanted + half * capacity).astype(BF16)
        picks.append(matmul(arrived, pick, ((0,), (0,))))
    for p in range(out_ref.shape[0]):
        out_ref[p] = jnp.where(wants_ref[p] == 1, picks[1], picks[0]).astype(BF16)


def mlp_kernel(rows_ref, up_ref, down_ref, out_ref):
    hidden_width = down_ref.shape[1]
    projected = matmul(up_ref[...], rows_ref[...])
    gate = projected[:hidden_width]
    hidden = (gate / (1.0 + jnp.exp(-gate)) * projected[hidden_width:]).astype(BF16)
    step = out_ref.shape[0] // 4
    for c in range(4):
        out_ref[c * step : (c + 1) * step, :] = matmul(
            down_ref[c * step : (c + 1) * step, :], hidden
        ).astype(BF16)


def merge_kernel(capacity, wants_ref, returned_ref, out_ref):
    pieces, part, rows = returned_ref.shape
    sums = [jnp.zeros((part, rows), F32), jnp.zeros((part, rows), F32)]
    for p in range(pieces):
        value = returned_ref[p].astype(F32)
        second = wants_ref[p] == 1
        sums[0] = sums[0] + jnp.where(second, 0.0, value)
        sums[1] = sums[1] + jnp.where(second, value, 0.0)
    target = lax.broadcasted_iota(I32, (2 * rows, rows), 0)
    row = lax.broadcasted_iota(I32, (2 * rows, rows), 1)
    home = row // capacity * (2 * capacity) + row % capacity
    result = jnp.zeros((2 * rows, part), F32)
    for half in range(2):
        put = (target == home + half * capacity).astype(BF16)
        result = result + matmul(put, sums[half].astype(BF16), ((1,), (1,)))
    out_ref[...] = result.astype(BF16)


def combine_kernel(xh_ref, weight_ref, back_ref, kept_ref, sent_ref):
    tok_rows = kept_ref.shape[0]
    for u, ref in ((xh_ref[0], kept_ref), (1 - xh_ref[0], sent_ref)):
        both = matmul(weight_ref[...], back_ref[u])
        ref[...] = both[:tok_rows] + both[tok_rows:]


def shaped(shape, dtype):
    return jax.ShapeDtypeStruct(shape, dtype)


def per_device(tokens, gate_scores, routes, balanced, gate_up, down_proj):
    split = lax.axis_size("e")
    lines = lax.axis_size("z")
    pieces = 2 * split
    tok_rows, top_count = routes.shape
    width = tokens.shape[1]
    part = width // pieces
    hidden_width = down_proj.shape[2]
    expert_count = 2 * 2 * lines
    capacity = min(tok_rows, max(2, 2 * tok_rows * top_count // expert_count))
    rows = 2 * lines * capacity
    xh, e, z = (lax.axis_index(n) for n in ("xh", "e", "z"))
    side = xh.astype(I32).reshape(1)
    near = ("yh", "e")
    far = ("yh", "z")

    mine = jnp.stack(
        [lax.dynamic_slice_in_dim(tokens, (e + u * split) * part, part, 1) for u in range(2)]
    )
    outgoing, weight = pl.pallas_call(
        lambda *refs: dispatch_kernel(lines, capacity, *refs),
        out_shape=(shaped((2, rows, part), BF16), shaped((2 * tok_rows, rows), BF16)),
        in_specs=[SMEM, VMEM, VMEM, VMEM],
        out_specs=(VMEM, VMEM),
        compiler_params=PARAMS,
        name="dispatch",
    )(side, routes, gate_scores, mine)
    outgoing = outgoing.reshape(2 * lines, 2 * capacity, part)
    arrived = lax.all_to_all(outgoing, far, split_axis=0, concat_axis=0, tiled=True)

    own_flag = lax.dynamic_index_in_dim(balanced[:, 0], z, 0, keepdims=True)
    flags = lax.all_gather(own_flag, "e", axis=0, tiled=True)
    wants = jnp.concatenate([flags, 1 - flags])
    spread = pl.pallas_call(
        lambda *refs: spread_kernel(capacity, *refs),
        out_shape=shaped((pieces, part, rows), BF16),
        in_specs=[SMEM, VMEM],
        out_specs=VMEM,
        compiler_params=PARAMS,
        name="spread",
    )(wants, arrived.reshape(2 * rows, part))
    gathered = lax.all_to_all(spread, near, split_axis=0, concat_axis=0, tiled=True)

    partial_value = pl.pallas_call(
        mlp_kernel,
        out_shape=shaped((width, rows), BF16),
        in_specs=[VMEM, VMEM, VMEM],
        out_specs=VMEM,
        compiler_params=PARAMS,
        name="tile_mlp",
    )(gathered.reshape(width, rows), gate_up[0, 0].T, down_proj[0, 0].T)
    returned = lax.all_to_all(
        partial_value.reshape(pieces, part, rows), near, split_axis=0, concat_axis=0, tiled=True
    )

    both = pl.pallas_call(
        lambda *refs: merge_kernel(capacity, *refs),
        out_shape=shaped((2 * rows, part), BF16),
        in_specs=[SMEM, VMEM],
        out_specs=VMEM,
        compiler_params=PARAMS,
        name="merge",
    )(wants, returned)
    both = both.reshape(2 * lines, 2 * capacity, part)
    back = lax.all_to_all(both, far, split_axis=0, concat_axis=0, tiled=True)

    kept, sent = pl.pallas_call(
        combine_kernel,
        out_shape=(shaped((tok_rows, part), F32), shaped((tok_rows, part), F32)),
        in_specs=[SMEM, VMEM, VMEM],
        out_specs=(VMEM, VMEM),
        compiler_params=PARAMS,
        name="combine",
    )(side, weight, back.reshape(2, rows, part))
    return kept + lax.ppermute(sent, "xh", [(0, 1), (1, 0)])


def solution(mesh):
    ep, dp = mesh.shape["ep"], mesh.shape["dp"]
    fine = Mesh(mesh.devices.reshape(2, ep // 2, 2, dp // 2), AXES)
    tok, exp = ("yh", "z"), ("xh", "e")
    placed = (
        P(tok, None),
        P(tok, None),
        P(tok, None),
        P(None, exp),
        P(tok, exp, None, None),
        P(tok, exp, None, None),
    )
    return jax.shard_map(
        per_device, mesh=fine, in_specs=placed, out_specs=P(tok, exp), check_vma=False
    )
```

```python
import jax
import jax.numpy as jnp
from jax import lax
from jax.experimental import pallas as pl
from jax.experimental.pallas import tpu as pltpu
from jax.sharding import Mesh, PartitionSpec as P

ROUTE_SCALE = 2.5
AXES = ("xh", "e", "yh", "z")
PLANE = ("yh", "xh", "e")
BF16, F32, I32 = jnp.bfloat16, jnp.float32, jnp.int32
SMEM = pl.BlockSpec(memory_space=pltpu.SMEM)
VMEM = pl.BlockSpec(memory_space=pltpu.VMEM)
PARAMS = pltpu.CompilerParams(vmem_limit_bytes=40 * 2**20)


def matmul(a, b, dims=((1,), (0,))):
    return lax.dot_general(a, b, (dims, ((), ())), preferred_element_type=F32)


def earlier(count):
    return (
        lax.broadcasted_iota(I32, (count, count), 0) > lax.broadcasted_iota(I32, (count, count), 1)
    ).astype(BF16)


def pack_kernel(expert_count, routes_ref, mine_ref, out_ref):
    tok_rows, top_count = routes_ref.shape
    part = mine_ref.shape[1]
    routes = routes_ref[...]
    expert = lax.broadcasted_iota(I32, (tok_rows, expert_count), 1)
    member = jnp.zeros((tok_rows, expert_count), F32)
    for k in range(top_count):
        member = jnp.where(routes[:, k : k + 1] == expert, 1.0, member)
    count = matmul(earlier(tok_rows), member.astype(BF16))
    lane = lax.broadcasted_iota(I32, (tok_rows, out_ref.shape[1] - part), 1)
    extra = jnp.zeros(lane.shape, F32)
    for k in range(top_count):
        named = routes[:, k : k + 1]
        place = jnp.sum(jnp.where(named == expert, count, 0.0), axis=1, keepdims=True)
        extra = jnp.where(lane == k, named.astype(F32), extra)
        extra = jnp.where(lane == top_count + k, place, extra)
    out_ref[...] = jnp.concatenate([mine_ref[...], extra.astype(BF16)], axis=1)


def weight_kernel(lines, capacity, routes_ref, scores_ref, weight_ref):
    tok_rows, top_count = routes_ref.shape
    rows = lines * 4 * capacity
    column = lax.broadcasted_iota(I32, (tok_rows, rows), 1)
    place = column % capacity
    group = column // capacity % 4
    line = column // (4 * capacity)
    expert_at = (group // 2 * lines + line) * 2 + group % 2
    routes = routes_ref[...]
    scores = scores_ref[...]
    scaled = scores / jnp.sum(scores, axis=1, keepdims=True) * ROUTE_SCALE
    weight = jnp.zeros((tok_rows, rows), F32)
    member = jnp.zeros((tok_rows, rows), F32)
    for k in range(top_count):
        match = routes[:, k : k + 1] == expert_at
        member = jnp.where(match, 1.0, member)
        weight = jnp.where(match, scaled[:, k : k + 1], weight)
    rank = matmul(earlier(tok_rows), member.astype(BF16))
    weight = jnp.where(rank == place.astype(F32), weight, 0.0)
    high = weight.astype(BF16)
    weight_ref[:tok_rows, :] = high
    weight_ref[tok_rows:, :] = (weight - high.astype(F32)).astype(BF16)


def spread_kernel(lines, capacity, top_count, z_ref, flags_ref, packed_ref, out_ref):
    count = packed_ref.shape[0]
    tok_rows = count // lines
    columns = out_ref.shape[3]
    part = out_ref.shape[2]
    packed = packed_ref[...]
    extra = packed[:, part : part + 2 * top_count].astype(F32)
    first = (lax.broadcasted_iota(I32, (count, 1), 0) // tok_rows * capacity).astype(F32)
    column = lax.broadcasted_iota(I32, (count, columns), 1).astype(F32)
    picks = []
    for group in range(4):
        expert = ((group // 2 * lines + z_ref[0]) * 2 + group % 2).astype(F32)
        home = jnp.full((count, 1), -1.0, F32)
        for k in range(top_count):
            match = extra[:, k : k + 1] == expert
            home = jnp.where(match, first + extra[:, top_count + k : top_count + k + 1], home)
        picks.append((home == column).astype(BF16))
    rows = matmul(packed[:, :part], jnp.concatenate(picks, axis=1), ((0,), (0,))).astype(BF16)
    rows = [rows[:, g * columns : (g + 1) * columns] for g in range(4)]
    split = out_ref.shape[1] // 2
    for yh in range(2):
        for c in range(2 * split):
            own = flags_ref[c] == 0
            xh = c // split

            @pl.when(own)
            def _(yh=yh, c=c, xh=xh):
                out_ref[yh, c] = rows[2 * yh + xh]

            @pl.when(jnp.logical_not(own))
            def _(yh=yh, c=c, xh=xh):
                out_ref[yh, c] = rows[2 * (1 - yh) + xh]


def mlp_kernel(rows_ref, up_ref, down_ref, out_ref):
    width, hidden_width = down_ref.shape
    columns = rows_ref.shape[2]
    rows = jnp.concatenate([rows_ref[0], rows_ref[1]], axis=1)
    projected = matmul(up_ref[...], rows)
    gate = projected[:hidden_width]
    hidden = (gate / (1.0 + jnp.exp(-gate)) * projected[hidden_width:]).astype(BF16)
    step = width // 4
    for c in range(4):
        here = slice(c * step, (c + 1) * step)
        value = matmul(down_ref[here, :], hidden).astype(BF16)
        out_ref[0, here, :] = value[:, :columns]
        out_ref[1, here, :] = value[:, columns:]


def merge_kernel(capacity, flags_ref, returned_ref, out_ref):
    halves, slots, part, columns = returned_ref.shape
    split = slots // 2
    sums = []
    for group in range(4):
        home, xh = group // 2, group % 2
        total = jnp.zeros((part, columns), F32)
        for c in range(xh * split, (xh + 1) * split):
            source = home ^ flags_ref[c]
            total = total + returned_ref[source, c].astype(F32)
        sums.append(total.astype(BF16))
    target = lax.broadcasted_iota(I32, (4 * columns, 4 * columns), 0)
    held = lax.broadcasted_iota(I32, (4 * columns, 4 * columns), 1)
    group, column = held // columns, held % columns
    home = column // capacity * (4 * capacity) + group * capacity + column % capacity
    put = (target == home).astype(BF16)
    out_ref[...] = matmul(put, jnp.concatenate(sums, axis=1), ((1,), (1,))).astype(BF16)


def combine_kernel(weight_ref, back_ref, mixed_ref):
    tok_rows = mixed_ref.shape[0]
    both = matmul(weight_ref[...], back_ref[...])
    mixed_ref[...] = both[:tok_rows] + both[tok_rows:]


def call(name, kernel, shape, dtype, specs, *args):
    return pl.pallas_call(
        kernel,
        out_shape=jax.ShapeDtypeStruct(shape, dtype),
        in_specs=specs,
        out_specs=VMEM,
        compiler_params=PARAMS,
        name=name,
    )(*args)


def per_device(tokens, gate_scores, routes, balanced, gate_up, down_proj):
    split = lax.axis_size("e")
    lines = lax.axis_size("z")
    slots = 2 * split
    tok_rows, top_count = routes.shape
    width = tokens.shape[1]
    part = width // slots
    expert_count = 4 * lines
    capacity = min(tok_rows, max(2, 2 * tok_rows * top_count // expert_count))
    columns = lines * capacity
    xh, e, z = (lax.axis_index(n) for n in ("xh", "e", "z"))
    packed_width = -(-(part + 2 * top_count) // 128) * 128

    own_flag = lax.dynamic_index_in_dim(balanced[:, 0], z, 0, keepdims=True)
    flags = lax.all_gather(own_flag, ("xh", "e"), axis=0, tiled=True)

    mine = lax.dynamic_slice_in_dim(tokens, (xh * split + e) * part, part, 1)
    packed = call(
        "pack",
        lambda *refs: pack_kernel(expert_count, *refs),
        (tok_rows, packed_width),
        BF16,
        [VMEM, VMEM],
        routes,
        mine,
    )
    packed = lax.all_gather(packed, "z", axis=0, tiled=True)
    spread = call(
        "spread",
        lambda *refs: spread_kernel(lines, capacity, top_count, *refs),
        (2, slots, part, columns),
        BF16,
        [SMEM, SMEM, VMEM],
        z.astype(I32).reshape(1),
        flags,
        packed,
    )
    spread = spread.reshape(2 * slots, part, columns)
    gathered = lax.all_to_all(spread, PLANE, split_axis=0, concat_axis=0, tiled=True)
    partial_value = call(
        "tile_mlp",
        mlp_kernel,
        (2, width, columns),
        BF16,
        [VMEM, VMEM, VMEM],
        gathered.reshape(2, width, columns),
        gate_up[0, 0].T,
        down_proj[0, 0].T,
    )
    partial_value = partial_value.reshape(2 * slots, part, columns)
    returned = lax.all_to_all(partial_value, PLANE, split_axis=0, concat_axis=0, tiled=True)
    merged = call(
        "merge",
        lambda *refs: merge_kernel(capacity, *refs),
        (4 * columns, part),
        BF16,
        [SMEM, VMEM],
        flags,
        returned.reshape(2, slots, part, columns),
    )
    merged = merged.reshape(lines, 4 * capacity, part)
    back = lax.all_to_all(merged, "z", split_axis=0, concat_axis=0, tiled=True)
    weight = call(
        "weight",
        lambda *refs: weight_kernel(lines, capacity, *refs),
        (2 * tok_rows, 4 * columns),
        BF16,
        [VMEM, VMEM],
        routes,
        gate_scores,
    )
    return call(
        "combine",
        combine_kernel,
        (tok_rows, part),
        F32,
        [VMEM, VMEM],
        weight,
        back.reshape(4 * columns, part),
    )


def solution(mesh):
    ep, dp = mesh.shape["ep"], mesh.shape["dp"]
    fine = Mesh(mesh.devices.reshape(2, ep // 2, 2, dp // 2), AXES)
    tok, exp = ("yh", "z"), ("xh", "e")
    placed = (
        P(tok, None),
        P(tok, None),
        P(tok, None),
        P(None, exp),
        P(tok, exp, None, None),
        P(tok, exp, None, None),
    )
    return jax.shard_map(
        per_device, mesh=fine, in_specs=placed, out_specs=P(tok, exp), check_vma=False
    )
```

```python
import jax
import jax.numpy as jnp
from jax import lax
from jax.experimental import pallas as pl
from jax.experimental.pallas import tpu as pltpu
from jax.sharding import Mesh, PartitionSpec as P

ROUTE_SCALE = 2.5
AXES = ("xh", "e", "yh", "zh", "zl")
PLANE = ("yh", "xh", "e")
BF16, F32, I32 = jnp.bfloat16, jnp.float32, jnp.int32
SMEM = pl.BlockSpec(memory_space=pltpu.SMEM)
VMEM = pl.BlockSpec(memory_space=pltpu.VMEM)
PARAMS = pltpu.CompilerParams(vmem_limit_bytes=40 * 2**20)


def matmul(a, b, dims=((1,), (0,))):
    return lax.dot_general(a, b, (dims, ((), ())), preferred_element_type=F32)


def pack_kernel(routes_ref, scores_ref, mine_ref, out_ref):
    tok_rows, top_count = routes_ref.shape
    part = mine_ref.shape[1]
    scores = scores_ref[...]
    scaled = scores / jnp.sum(scores, axis=1, keepdims=True) * ROUTE_SCALE
    high = scaled.astype(BF16).astype(F32)
    low = scaled - high
    named = routes_ref[...].astype(F32)
    lane = lax.broadcasted_iota(I32, (tok_rows, out_ref.shape[1] - part), 1)
    extra = jnp.zeros(lane.shape, F32)
    for k in range(top_count):
        extra = jnp.where(lane == k, named[:, k : k + 1], extra)
        extra = jnp.where(lane == top_count + k, high[:, k : k + 1], extra)
        extra = jnp.where(lane == 2 * top_count + k, low[:, k : k + 1], extra)
    out_ref[...] = jnp.concatenate([mine_ref[...], extra.astype(BF16)], axis=1)


def choice(shape, zh, capacity, extra, top_count, with_weight):
    high_lines, low_lines = shape
    lines = high_lines * low_lines
    count = extra.shape[0]
    tok_rows = count // high_lines
    columns = lines * 4 * capacity
    column = lax.broadcasted_iota(I32, (1, columns), 1)
    place = column % capacity
    group = column // capacity % 4
    block = column // (4 * capacity) % high_lines
    low_line = column // (4 * capacity * high_lines)
    expert_at = ((group // 2 * lines + zh * low_lines + low_line) * 2 + group % 2).astype(F32)
    row = lax.broadcasted_iota(I32, (count, 1), 0)
    member = jnp.zeros((count, columns), F32)
    weight = jnp.zeros((count, columns), F32)
    for k in range(top_count):
        match = extra[:, k : k + 1] == expert_at
        member = jnp.where(match, 1.0, member)
        if with_weight:
            scaled = (
                extra[:, top_count + k : top_count + k + 1]
                + extra[:, 2 * top_count + k : 2 * top_count + k + 1]
            )
            weight = jnp.where(match, scaled, weight)
    after = lax.broadcasted_iota(I32, (count, count), 0)
    first = lax.broadcasted_iota(I32, (count, count), 1)
    before = ((after > first) & (after // tok_rows == first // tok_rows)).astype(BF16)
    rank = matmul(before, member.astype(BF16))
    chosen = (rank == place.astype(F32)) & (row // tok_rows == block)
    return jnp.where(chosen, weight if with_weight else member, 0.0)


def select_kernel(shape, capacity, top_count, zh_ref, packed_ref, out_ref):
    part = out_ref.shape[1]
    packed = packed_ref[...]
    extra = packed[:, part : part + 3 * top_count].astype(F32)
    member = choice(shape, zh_ref[0], capacity, extra, top_count, False)
    out_ref[...] = matmul(member.astype(BF16), packed[:, :part], ((0,), (0,))).astype(BF16)


def weight_kernel(shape, capacity, top_count, part, zh_ref, packed_ref, weight_ref):
    count = packed_ref.shape[0]
    extra = packed_ref[:, part : part + 3 * top_count].astype(F32)
    weight = choice(shape, zh_ref[0], capacity, extra, top_count, True)
    high = weight.astype(BF16)
    weight_ref[:count, :] = high
    weight_ref[count:, :] = (weight - high.astype(F32)).astype(BF16)


def spread_kernel(capacity, flags_ref, arrived_ref, out_ref):
    total = arrived_ref.shape[0]
    columns = out_ref.shape[3]
    source = lax.broadcasted_iota(I32, (total, total), 0)
    target = lax.broadcasted_iota(I32, (total, total), 1)
    group, column = target // columns, target % columns
    home = column // capacity * (4 * capacity) + group * capacity + column % capacity
    pick = (source == home).astype(BF16)
    rows = matmul(arrived_ref[...], pick, ((0,), (0,))).astype(BF16)
    rows = [rows[:, g * columns : (g + 1) * columns] for g in range(4)]
    split = out_ref.shape[1] // 2
    for c in range(2 * split):
        xh = c // split
        swap = flags_ref[c]
        out_ref[swap, c] = rows[xh]
        out_ref[1 - swap, c] = rows[2 + xh]


def mlp_kernel(rows_ref, up_ref, down_ref, out_ref):
    width, hidden_width = down_ref.shape
    columns = rows_ref.shape[2]
    rows = jnp.concatenate([rows_ref[0], rows_ref[1]], axis=1)
    projected = matmul(up_ref[...], rows)
    gate = projected[:hidden_width]
    hidden = (gate / (1.0 + jnp.exp(-gate)) * projected[hidden_width:]).astype(BF16)
    step = width // 4
    for c in range(4):
        here = slice(c * step, (c + 1) * step)
        value = matmul(down_ref[here, :], hidden).astype(BF16)
        out_ref[0, here, :] = value[:, :columns]
        out_ref[1, here, :] = value[:, columns:]


def merge_kernel(capacity, flags_ref, returned_ref, out_ref):
    halves, slots, part, columns = returned_ref.shape
    split = slots // 2
    sums = []
    for group in range(4):
        home, xh = group // 2, group % 2
        total = jnp.zeros((part, columns), F32)
        for c in range(xh * split, (xh + 1) * split):
            source = home ^ flags_ref[c]
            total = total + returned_ref[source, c].astype(F32)
        sums.append(total.astype(BF16))
    target = lax.broadcasted_iota(I32, (4 * columns, 4 * columns), 0)
    held = lax.broadcasted_iota(I32, (4 * columns, 4 * columns), 1)
    group, column = held // columns, held % columns
    home = column // capacity * (4 * capacity) + group * capacity + column % capacity
    put = (target == home).astype(BF16)
    out_ref[...] = matmul(put, jnp.concatenate(sums, axis=1), ((1,), (1,))).astype(BF16)


def combine_kernel(weight_ref, back_ref, mixed_ref):
    count = mixed_ref.shape[0]
    both = matmul(weight_ref[...], back_ref[...])
    mixed_ref[...] = (both[:count] + both[count:]).astype(BF16)


def call(name, kernel, shape, dtype, specs, *args):
    return pl.pallas_call(
        kernel,
        out_shape=jax.ShapeDtypeStruct(shape, dtype),
        in_specs=specs,
        out_specs=VMEM,
        compiler_params=PARAMS,
        name=name,
    )(*args)


def per_device(tokens, gate_scores, routes, balanced, gate_up, down_proj):
    split = lax.axis_size("e")
    shape = lax.axis_size("zh"), lax.axis_size("zl")
    lines = shape[0] * shape[1]
    slots = 2 * split
    tok_rows, top_count = routes.shape
    width = tokens.shape[1]
    part = width // slots
    expert_count = 4 * lines
    capacity = min(tok_rows, max(2, 2 * tok_rows * top_count // expert_count))
    columns = lines * capacity
    xh, e, zh, zl = (lax.axis_index(n) for n in ("xh", "e", "zh", "zl"))
    packed_width = -(-(part + 3 * top_count) // 128) * 128
    level = zh.astype(I32).reshape(1)

    mine = lax.dynamic_slice_in_dim(tokens, (xh * split + e) * part, part, 1)
    packed = call(
        "pack",
        pack_kernel,
        (tok_rows, packed_width),
        BF16,
        [VMEM, VMEM, VMEM],
        routes,
        gate_scores,
        mine,
    )
    packed = lax.all_gather(packed, "zh", axis=0, tiled=True)
    outgoing = call(
        "select",
        lambda *refs: select_kernel(shape, capacity, top_count, *refs),
        (4 * columns, part),
        BF16,
        [SMEM, VMEM],
        level,
        packed,
    )
    outgoing = outgoing.reshape(shape[1], 4 * columns // shape[1], part)
    arrived = lax.all_to_all(outgoing, "zl", split_axis=0, concat_axis=0, tiled=True)
    own_flag = lax.dynamic_index_in_dim(
        balanced[:, 0], zh * shape[1] + zl, 0, keepdims=True
    )
    flags = lax.all_gather(own_flag, ("xh", "e"), axis=0, tiled=True)
    weight = call(
        "weight",
        lambda *refs: weight_kernel(shape, capacity, top_count, part, *refs),
        (2 * shape[0] * tok_rows, 4 * columns),
        BF16,
        [SMEM, VMEM],
        level,
        packed,
    )
    spread = call(
        "spread",
        lambda *refs: spread_kernel(capacity, *refs),
        (2, slots, part, columns),
        BF16,
        [SMEM, VMEM],
        flags,
        arrived.reshape(4 * columns, part),
    )
    spread = spread.reshape(2 * slots, part, columns)
    gathered = lax.all_to_all(spread, PLANE, split_axis=0, concat_axis=0, tiled=True)
    partial_value = call(
        "tile_mlp",
        mlp_kernel,
        (2, width, columns),
        BF16,
        [VMEM, VMEM, VMEM],
        gathered.reshape(2, width, columns),
        gate_up[0, 0].T,
        down_proj[0, 0].T,
    )
    partial_value = partial_value.reshape(2 * slots, part, columns)
    returned = lax.all_to_all(partial_value, PLANE, split_axis=0, concat_axis=0, tiled=True)
    merged = call(
        "merge",
        lambda *refs: merge_kernel(capacity, *refs),
        (4 * columns, part),
        BF16,
        [SMEM, VMEM],
        flags,
        returned.reshape(2, slots, part, columns),
    )
    merged = merged.reshape(shape[1], 4 * columns // shape[1], part)
    back = lax.all_to_all(merged, "zl", split_axis=0, concat_axis=0, tiled=True)
    mixed = call(
        "combine",
        combine_kernel,
        (shape[0] * tok_rows, part),
        BF16,
        [VMEM, VMEM],
        weight,
        back.reshape(4 * columns, part),
    )
    mixed = mixed.reshape(shape[0], tok_rows, part)
    mixed = lax.all_to_all(mixed, "zh", split_axis=0, concat_axis=0, tiled=True)
    return jnp.sum(mixed.astype(F32), axis=0)


def solution(mesh):
    ep, dp = mesh.shape["ep"], mesh.shape["dp"]
    low = dp // 8
    fine = Mesh(mesh.devices.reshape(2, ep // 2, 2, dp // 2 // low, low), AXES)
    tok, exp = ("yh", "zh", "zl"), ("xh", "e")
    placed = (
        P(tok, None),
        P(tok, None),
        P(tok, None),
        P(None, exp),
        P(tok, exp, None, None),
        P(tok, exp, None, None),
    )
    return jax.shard_map(
        per_device, mesh=fine, in_specs=placed, out_specs=P(tok, exp), check_vma=False
    )
```

```python
import jax
import jax.numpy as jnp
from jax import lax
from jax.experimental import pallas as pl
from jax.experimental.pallas import tpu as pltpu
from jax.sharding import Mesh, PartitionSpec as P

ROUTE_SCALE = 2.5
CHUNKS = 1
AXES = ("xh", "e", "yh", "z")
PLANE = ("yh", "xh", "e")
BF16, F32, I32 = jnp.bfloat16, jnp.float32, jnp.int32
SMEM = pl.BlockSpec(memory_space=pltpu.SMEM)
VMEM = pl.BlockSpec(memory_space=pltpu.VMEM)
PARAMS = pltpu.CompilerParams(vmem_limit_bytes=24 * 2**20)


def matmul(a, b, dims=((1,), (0,))):
    return lax.dot_general(a, b, (dims, ((), ())), preferred_element_type=F32)


def earlier(count):
    return (
        lax.broadcasted_iota(I32, (count, count), 0) > lax.broadcasted_iota(I32, (count, count), 1)
    ).astype(BF16)


def column_of(lines, capacity, shape):
    column = lax.broadcasted_iota(I32, shape, 1)
    group = column // capacity % 4
    line = column // (4 * capacity)
    return (group // 2 * lines + line) * 2 + group % 2, column % capacity


def dispatch_kernel(lines, capacity, routes_ref, mine_ref, *out_refs):
    top_count, tok_rows = routes_ref.shape
    rows = lines * 4 * capacity
    expert_at, place = column_of(lines, capacity, (1, rows))
    unit = (
        lax.broadcasted_iota(I32, (top_count, top_count), 0)
        == lax.broadcasted_iota(I32, (top_count, top_count), 1)
    ).astype(BF16)
    routes = matmul(routes_ref[...].astype(F32).astype(BF16), unit, ((0,), (0,)))
    member = jnp.zeros((tok_rows, rows), F32)
    for k in range(top_count):
        member = jnp.where(routes[:, k : k + 1] == expert_at.astype(F32), 1.0, member)
    rank = matmul(earlier(tok_rows), member.astype(BF16))
    chosen = jnp.where(rank == place.astype(F32), member, 0.0).astype(BF16)
    value = matmul(chosen, mine_ref[...], ((0,), (0,))).astype(BF16)
    step = value.shape[1] // len(out_refs)
    for h, out_ref in enumerate(out_refs):
        out_ref[...] = value[:, h * step : (h + 1) * step]


def weight_kernel(lines, capacity, routes_ref, scores_ref, weight_ref):
    tok_rows, top_count = routes_ref.shape
    rows = lines * 4 * capacity
    expert_at, place = column_of(lines, capacity, (1, rows))
    routes = routes_ref[...]
    scores = scores_ref[...]
    scaled = scores / jnp.sum(scores, axis=1, keepdims=True) * ROUTE_SCALE
    weight = jnp.zeros((tok_rows, rows), F32)
    member = jnp.zeros((tok_rows, rows), F32)
    for k in range(top_count):
        match = routes[:, k : k + 1] == expert_at
        member = jnp.where(match, 1.0, member)
        weight = jnp.where(match, scaled[:, k : k + 1], weight)
    rank = matmul(earlier(tok_rows), member.astype(BF16))
    weight = jnp.where(rank == place.astype(F32), weight, 0.0)
    high = weight.astype(BF16)
    weight_ref[:tok_rows, :] = high
    weight_ref[tok_rows:, :] = (weight - high.astype(F32)).astype(BF16)


def spread_kernel(capacity, flags_ref, arrived_ref, out_ref):
    total = arrived_ref.shape[0]
    columns = out_ref.shape[3]
    source = lax.broadcasted_iota(I32, (total, total), 0)
    target = lax.broadcasted_iota(I32, (total, total), 1)
    group, column = target // columns, target % columns
    home = column // capacity * (4 * capacity) + group * capacity + column % capacity
    pick = (source == home).astype(BF16)
    rows = matmul(arrived_ref[...], pick, ((0,), (0,))).astype(BF16)
    rows = [rows[:, g * columns : (g + 1) * columns] for g in range(4)]
    split = out_ref.shape[1] // 2
    for c in range(2 * split):
        xh = c // split
        swap = flags_ref[c]
        out_ref[swap, c] = rows[xh]
        out_ref[1 - swap, c] = rows[2 + xh]


def mlp_kernel(chunks, *refs):
    rows_refs, up_refs, down_refs, out_refs = (
        refs[i * chunks : (i + 1) * chunks] for i in range(4)
    )
    hidden_width = down_refs[0].shape[1]
    columns = rows_refs[0].shape[2]
    projected = 0.0
    for rows_ref, up_ref in zip(rows_refs, up_refs):
        rows = jnp.concatenate([rows_ref[0], rows_ref[1]], axis=1)
        projected = projected + matmul(up_ref[...], rows)
    gate = projected[:hidden_width]
    hidden = (gate / (1.0 + jnp.exp(-gate)) * projected[hidden_width:]).astype(BF16)
    for down_ref, out_ref in zip(down_refs, out_refs):
        step = down_ref.shape[0] // 2
        for c in range(2):
            here = slice(c * step, (c + 1) * step)
            value = matmul(down_ref[here, :], hidden).astype(BF16)
            out_ref[0, here, :] = value[:, :columns]
            out_ref[1, here, :] = value[:, columns:]


def merge_kernel(capacity, flags_ref, returned_ref, out_ref):
    halves, slots, part, columns = returned_ref.shape
    split = slots // 2
    sums = []
    for group in range(4):
        home, xh = group // 2, group % 2
        total = jnp.zeros((part, columns), F32)
        for c in range(xh * split, (xh + 1) * split):
            source = home ^ flags_ref[c]
            total = total + returned_ref[source, c].astype(F32)
        sums.append(total.astype(BF16))
    target = lax.broadcasted_iota(I32, (4 * columns, 4 * columns), 0)
    held = lax.broadcasted_iota(I32, (4 * columns, 4 * columns), 1)
    group, column = held // columns, held % columns
    home = column // capacity * (4 * capacity) + group * capacity + column % capacity
    put = (target == home).astype(BF16)
    out_ref[...] = matmul(put, jnp.concatenate(sums, axis=1), ((1,), (1,))).astype(BF16)


def combine_kernel(weight_ref, *refs):
    back_refs, mixed_ref = refs[:-1], refs[-1]
    tok_rows = mixed_ref.shape[0]
    pieces = []
    for back_ref in back_refs:
        both = matmul(weight_ref[...], back_ref[...])
        pieces.append(both[:tok_rows] + both[tok_rows:])
    mixed_ref[...] = jnp.concatenate(pieces, axis=1)


def call(name, kernel, shape, dtype, specs, *args, copies=0):
    one = jax.ShapeDtypeStruct(shape, dtype)
    return pl.pallas_call(
        kernel,
        out_shape=(one,) * copies if copies else one,
        in_specs=specs,
        out_specs=(VMEM,) * copies if copies else VMEM,
        compiler_params=PARAMS,
        name=name,
    )(*args)


def swap(value, axes):
    return lax.all_to_all(value, axes, split_axis=0, concat_axis=0, tiled=True)


def per_device(tokens, gate_scores, routes, balanced, gate_up, down_proj):
    split = lax.axis_size("e")
    lines = lax.axis_size("z")
    slots = 2 * split
    tok_rows, top_count = routes.shape
    width = tokens.shape[1]
    hidden_width = down_proj.shape[2]
    part = width // slots
    step = part // CHUNKS
    expert_count = 4 * lines
    capacity = min(tok_rows, max(2, 2 * tok_rows * top_count // expert_count))
    columns = lines * capacity
    xh, e, z = (lax.axis_index(n) for n in ("xh", "e", "z"))
    every = range(CHUNKS)

    mine = lax.dynamic_slice_in_dim(tokens, (xh * split + e) * part, part, 1)
    outgoing = call(
        "dispatch",
        lambda *refs: dispatch_kernel(lines, capacity, *refs),
        (4 * columns, step),
        BF16,
        [VMEM, VMEM],
        routes.T,
        mine,
        copies=CHUNKS,
    )
    arrived = [swap(v.reshape(lines, 4 * capacity, step), "z") for v in outgoing]
    own_flag = lax.dynamic_index_in_dim(balanced[:, 0], z, 0, keepdims=True)
    flags = lax.all_gather(own_flag, ("xh", "e"), axis=0, tiled=True)
    gathered = []
    for v in arrived:
        spread = call(
            "spread",
            lambda *refs: spread_kernel(capacity, *refs),
            (2, slots, step, columns),
            BF16,
            [SMEM, VMEM],
            flags,
            v.reshape(4 * columns, step),
        )
        v = swap(spread.reshape(2 * slots, step, columns), PLANE)
        gathered.append(v.reshape(2, slots * step, columns))
    up = gate_up[0, 0].reshape(slots, CHUNKS, step, 2 * hidden_width)
    up = [up[:, h].reshape(slots * step, 2 * hidden_width).T for h in every]
    down = down_proj[0, 0].reshape(hidden_width, slots, CHUNKS, step)
    down = [down[:, :, h].reshape(hidden_width, slots * step).T for h in every]
    partial_value = call(
        "tile_mlp",
        lambda *refs: mlp_kernel(CHUNKS, *refs),
        (2, slots * step, columns),
        BF16,
        [VMEM] * (3 * CHUNKS),
        *gathered,
        *up,
        *down,
        copies=CHUNKS,
    )
    back = []
    for v in partial_value:
        returned = swap(v.reshape(2 * slots, step, columns), PLANE)
        merged = call(
            "merge",
            lambda *refs: merge_kernel(capacity, *refs),
            (4 * columns, step),
            BF16,
            [SMEM, VMEM],
            flags,
            returned.reshape(2, slots, step, columns),
        )
        merged = swap(merged.reshape(lines, 4 * capacity, step), "z")
        back.append(merged.reshape(4 * columns, step))
    weight = call(
        "weight",
        lambda *refs: weight_kernel(lines, capacity, *refs),
        (2 * tok_rows, 4 * columns),
        BF16,
        [VMEM, VMEM],
        routes,
        gate_scores,
    )
    return call(
        "combine", combine_kernel, (tok_rows, part), F32, [VMEM] * (1 + CHUNKS), weight, *back
    )


def solution(mesh):
    ep, dp = mesh.shape["ep"], mesh.shape["dp"]
    fine = Mesh(mesh.devices.reshape(2, ep // 2, 2, dp // 2), AXES)
    tok, exp = ("yh", "z"), ("xh", "e")
    placed = (
        P(tok, None),
        P(tok, None),
        P(tok, None),
        P(None, exp),
        P(tok, exp, None, None),
        P(tok, exp, None, None),
    )
    return jax.shard_map(
        per_device, mesh=fine, in_specs=placed, out_specs=P(tok, exp), check_vma=False
    )
```

```python
import jax
import jax.numpy as jnp
from jax import lax
from jax.experimental import pallas as pl
from jax.experimental.pallas import tpu as pltpu
from jax.sharding import Mesh, PartitionSpec as P

ROUTE_SCALE = 2.5
CHUNKS = 1
AXES = ("xh", "e", "yh", "z")
PLANE = ("yh", "xh", "e")
BF16, F32, I32 = jnp.bfloat16, jnp.float32, jnp.int32
SMEM = pl.BlockSpec(memory_space=pltpu.SMEM)
VMEM = pl.BlockSpec(memory_space=pltpu.VMEM)
PARAMS = pltpu.CompilerParams(vmem_limit_bytes=24 * 2**20)


def matmul(a, b, dims=((1,), (0,))):
    return lax.dot_general(a, b, (dims, ((), ())), preferred_element_type=F32)


def earlier(count):
    return (
        lax.broadcasted_iota(I32, (count, count), 0) > lax.broadcasted_iota(I32, (count, count), 1)
    ).astype(BF16)


def column_of(lines, capacity, shape):
    column = lax.broadcasted_iota(I32, shape, 1)
    group = column // capacity % 4
    line = column // (4 * capacity)
    return (group // 2 * lines + line) * 2 + group % 2, column % capacity


def dispatch_kernel(lines, capacity, routes_ref, mine_ref, *out_refs):
    top_count, tok_rows = routes_ref.shape
    rows = lines * 4 * capacity
    expert_at, place = column_of(lines, capacity, (1, rows))
    unit = (
        lax.broadcasted_iota(I32, (top_count, top_count), 0)
        == lax.broadcasted_iota(I32, (top_count, top_count), 1)
    ).astype(BF16)
    routes = matmul(routes_ref[...].astype(F32).astype(BF16), unit, ((0,), (0,)))
    member = jnp.zeros((tok_rows, rows), F32)
    for k in range(top_count):
        member = jnp.where(routes[:, k : k + 1] == expert_at.astype(F32), 1.0, member)
    rank = matmul(earlier(tok_rows), member.astype(BF16))
    chosen = jnp.where(rank == place.astype(F32), member, 0.0).astype(BF16)
    value = matmul(chosen, mine_ref[...], ((0,), (0,))).astype(BF16)
    step = value.shape[1] // len(out_refs)
    for h, out_ref in enumerate(out_refs):
        out_ref[...] = value[:, h * step : (h + 1) * step]


def weight_kernel(lines, capacity, routes_ref, scores_ref, weight_ref):
    tok_rows, top_count = routes_ref.shape
    rows = lines * 4 * capacity
    expert_at, place = column_of(lines, capacity, (1, rows))
    routes = routes_ref[...]
    scores = scores_ref[...]
    scaled = scores / jnp.sum(scores, axis=1, keepdims=True) * ROUTE_SCALE
    weight = jnp.zeros((tok_rows, rows), F32)
    member = jnp.zeros((tok_rows, rows), F32)
    for k in range(top_count):
        match = routes[:, k : k + 1] == expert_at
        member = jnp.where(match, 1.0, member)
        weight = jnp.where(match, scaled[:, k : k + 1], weight)
    rank = matmul(earlier(tok_rows), member.astype(BF16))
    weight = jnp.where(rank == place.astype(F32), weight, 0.0)
    high = weight.astype(BF16)
    weight_ref[:tok_rows, :] = high
    weight_ref[tok_rows:, :] = (weight - high.astype(F32)).astype(BF16)


def spread_kernel(capacity, flags_ref, arrived_ref, out_ref):
    total = arrived_ref.shape[0]
    columns = out_ref.shape[3]
    source = lax.broadcasted_iota(I32, (total, 1), 0)
    target = lax.broadcasted_iota(I32, (1, total), 1)
    group, column = target // columns, target % columns
    home = column // capacity * (4 * capacity) + group * capacity + column % capacity
    pick = (source == home).astype(BF16)
    rows = matmul(arrived_ref[...], pick, ((0,), (0,))).astype(BF16)
    rows = [rows[:, g * columns : (g + 1) * columns] for g in range(4)]
    split = out_ref.shape[1] // 2
    for c in range(2 * split):
        xh = c // split
        swap = flags_ref[c]
        out_ref[swap, c] = rows[xh]
        out_ref[1 - swap, c] = rows[2 + xh]


def mlp_kernel(chunks, *refs):
    rows_refs, up_refs, down_refs, out_refs = (
        refs[i * chunks : (i + 1) * chunks] for i in range(4)
    )
    hidden_width = down_refs[0].shape[1]
    columns = rows_refs[0].shape[2]
    projected = 0.0
    for rows_ref, up_ref in zip(rows_refs, up_refs):
        rows = jnp.concatenate([rows_ref[0], rows_ref[1]], axis=1)
        projected = projected + matmul(up_ref[...], rows)
    gate = projected[:hidden_width]
    hidden = (gate / (1.0 + jnp.exp(-gate)) * projected[hidden_width:]).astype(BF16)
    for down_ref, out_ref in zip(down_refs, out_refs):
        step = down_ref.shape[0] // 2
        for c in range(2):
            here = slice(c * step, (c + 1) * step)
            value = matmul(down_ref[here, :], hidden).astype(BF16)
            out_ref[0, here, :] = value[:, :columns]
            out_ref[1, here, :] = value[:, columns:]


def merge_kernel(capacity, flags_ref, returned_ref, out_ref):
    halves, slots, part, columns = returned_ref.shape
    split = slots // 2
    sums = []
    for group in range(4):
        home, xh = group // 2, group % 2
        total = jnp.zeros((part, columns), F32)
        for c in range(xh * split, (xh + 1) * split):
            source = home ^ flags_ref[c]
            total = total + returned_ref[source, c].astype(F32)
        sums.append(total.astype(BF16))
    target = lax.broadcasted_iota(I32, (4 * columns, 1), 0)
    held = lax.broadcasted_iota(I32, (1, 4 * columns), 1)
    group, column = held // columns, held % columns
    home = column // capacity * (4 * capacity) + group * capacity + column % capacity
    put = (target == home).astype(BF16)
    out_ref[...] = matmul(put, jnp.concatenate(sums, axis=1), ((1,), (1,))).astype(BF16)


def combine_kernel(weight_ref, *refs):
    back_refs, mixed_ref = refs[:-1], refs[-1]
    tok_rows = mixed_ref.shape[0]
    pieces = []
    for back_ref in back_refs:
        both = matmul(weight_ref[...], back_ref[...])
        pieces.append(both[:tok_rows] + both[tok_rows:])
    mixed_ref[...] = jnp.concatenate(pieces, axis=1)


def call(name, kernel, shape, dtype, specs, *args, copies=0):
    one = jax.ShapeDtypeStruct(shape, dtype)
    return pl.pallas_call(
        kernel,
        out_shape=(one,) * copies if copies else one,
        in_specs=specs,
        out_specs=(VMEM,) * copies if copies else VMEM,
        compiler_params=PARAMS,
        name=name,
    )(*args)


def swap(value, axes):
    return lax.all_to_all(value, axes, split_axis=0, concat_axis=0, tiled=True)


def per_device(tokens, gate_scores, routes, balanced, gate_up, down_proj):
    split = lax.axis_size("e")
    lines = lax.axis_size("z")
    slots = 2 * split
    tok_rows, top_count = routes.shape
    width = tokens.shape[1]
    hidden_width = down_proj.shape[2]
    part = width // slots
    step = part // CHUNKS
    expert_count = 4 * lines
    capacity = min(tok_rows, max(2, 2 * tok_rows * top_count // expert_count))
    columns = lines * capacity
    xh, e, z = (lax.axis_index(n) for n in ("xh", "e", "z"))
    every = range(CHUNKS)

    mine = lax.dynamic_slice_in_dim(tokens, (xh * split + e) * part, part, 1)
    outgoing = call(
        "dispatch",
        lambda *refs: dispatch_kernel(lines, capacity, *refs),
        (4 * columns, step),
        BF16,
        [VMEM, VMEM],
        routes.T,
        mine,
        copies=CHUNKS,
    )
    arrived = [swap(v.reshape(lines, 4 * capacity, step), "z") for v in outgoing]
    own_flag = lax.dynamic_index_in_dim(balanced[:, 0], z, 0, keepdims=True)
    flags = lax.all_gather(own_flag, ("xh", "e"), axis=0, tiled=True)
    weight = call(
        "weight",
        lambda *refs: weight_kernel(lines, capacity, *refs),
        (2 * tok_rows, 4 * columns),
        BF16,
        [VMEM, VMEM],
        routes,
        gate_scores,
    )
    up = gate_up[0, 0].reshape(slots, CHUNKS, step, 2 * hidden_width)
    up = [up[:, h].reshape(slots * step, 2 * hidden_width).T for h in every]
    down = down_proj[0, 0].reshape(hidden_width, slots, CHUNKS, step)
    down = [down[:, :, h].reshape(hidden_width, slots * step).T for h in every]
    arrived, up, down, weight = lax.optimization_barrier((arrived, up, down, weight))
    gathered = []
    for v in arrived:
        spread = call(
            "spread",
            lambda *refs: spread_kernel(capacity, *refs),
            (2, slots, step, columns),
            BF16,
            [SMEM, VMEM],
            flags,
            v.reshape(4 * columns, step),
        )
        v = swap(spread.reshape(2 * slots, step, columns), PLANE)
        gathered.append(v.reshape(2, slots * step, columns))
    partial_value = call(
        "tile_mlp",
        lambda *refs: mlp_kernel(CHUNKS, *refs),
        (2, slots * step, columns),
        BF16,
        [VMEM] * (3 * CHUNKS),
        *gathered,
        *up,
        *down,
        copies=CHUNKS,
    )
    back = []
    for v in partial_value:
        returned = swap(v.reshape(2 * slots, step, columns), PLANE)
        merged = call(
            "merge",
            lambda *refs: merge_kernel(capacity, *refs),
            (4 * columns, step),
            BF16,
            [SMEM, VMEM],
            flags,
            returned.reshape(2, slots, step, columns),
        )
        merged = swap(merged.reshape(lines, 4 * capacity, step), "z")
        back.append(merged.reshape(4 * columns, step))
    return call(
        "combine", combine_kernel, (tok_rows, part), F32, [VMEM] * (1 + CHUNKS), weight, *back
    )


def solution(mesh):
    ep, dp = mesh.shape["ep"], mesh.shape["dp"]
    fine = Mesh(mesh.devices.reshape(2, ep // 2, 2, dp // 2), AXES)
    tok, exp = ("yh", "z"), ("xh", "e")
    placed = (
        P(tok, None),
        P(tok, None),
        P(tok, None),
        P(None, exp),
        P(tok, exp, None, None),
        P(tok, exp, None, None),
    )
    return jax.shard_map(
        per_device, mesh=fine, in_specs=placed, out_specs=P(tok, exp), check_vma=False
    )
```

```python
import jax
import jax.numpy as jnp
from jax import lax
from jax.experimental import pallas as pl
from jax.experimental.pallas import tpu as pltpu
from jax.sharding import Mesh, PartitionSpec as P

ROUTE_SCALE = 2.5
AXES = ("xh", "e", "yh", "z")
PLANE = ("yh", "xh", "e")
BF16, F32, I32 = jnp.bfloat16, jnp.float32, jnp.int32
SMEM = pl.BlockSpec(memory_space=pltpu.SMEM)
VMEM = pl.BlockSpec(memory_space=pltpu.VMEM)
PARAMS = pltpu.CompilerParams(vmem_limit_bytes=24 * 2**20)


def matmul(a, b, dims=((1,), (0,))):
    return lax.dot_general(a, b, (dims, ((), ())), preferred_element_type=F32)


def earlier(count):
    return (
        lax.broadcasted_iota(I32, (count, count), 0) > lax.broadcasted_iota(I32, (count, count), 1)
    ).astype(BF16)


def column_of(lines, capacity, shape):
    column = lax.broadcasted_iota(I32, shape, 1)
    place = column // (4 * lines)
    line = column // 4 % lines
    group = column % 4
    return (group // 2 * lines + line) * 2 + group % 2, place


def fold(value, shape):
    places = shape[2] // value.shape[1]
    rows = value.shape[0] // places
    wide = [value[p * rows : (p + 1) * rows] for p in range(places)]
    return jnp.concatenate(wide, axis=1).reshape(shape).astype(BF16)


def unfold(value, places):
    lines, groups, width = value.shape
    flat = value.reshape(lines * groups, width)
    part = width // places
    return jnp.concatenate([flat[:, p * part : (p + 1) * part] for p in range(places)], axis=0)


def dispatch_kernel(lines, capacity, routes_ref, mine_ref, out_ref):
    top_count, tok_rows = routes_ref.shape
    rows = lines * 4 * capacity
    expert_at, place = column_of(lines, capacity, (1, rows))
    unit = (
        lax.broadcasted_iota(I32, (top_count, top_count), 0)
        == lax.broadcasted_iota(I32, (top_count, top_count), 1)
    ).astype(BF16)
    routes = matmul(routes_ref[...].astype(F32).astype(BF16), unit, ((0,), (0,)))
    member = jnp.zeros((tok_rows, rows), F32)
    for k in range(top_count):
        member = jnp.where(routes[:, k : k + 1] == expert_at.astype(F32), 1.0, member)
    rank = matmul(earlier(tok_rows), member.astype(BF16))
    chosen = jnp.where(rank == place.astype(F32), member, 0.0).astype(BF16)
    out_ref[...] = fold(matmul(chosen, mine_ref[...], ((0,), (0,))), out_ref.shape)


def weight_kernel(lines, capacity, routes_ref, scores_ref, weight_ref):
    tok_rows, top_count = routes_ref.shape
    rows = lines * 4 * capacity
    expert_at, place = column_of(lines, capacity, (1, rows))
    routes = routes_ref[...]
    scores = scores_ref[...]
    scaled = scores / jnp.sum(scores, axis=1, keepdims=True) * ROUTE_SCALE
    weight = jnp.zeros((tok_rows, rows), F32)
    member = jnp.zeros((tok_rows, rows), F32)
    for k in range(top_count):
        match = routes[:, k : k + 1] == expert_at
        member = jnp.where(match, 1.0, member)
        weight = jnp.where(match, scaled[:, k : k + 1], weight)
    rank = matmul(earlier(tok_rows), member.astype(BF16))
    weight = jnp.where(rank == place.astype(F32), weight, 0.0)
    high = weight.astype(BF16)
    weight_ref[:tok_rows, :] = high
    weight_ref[tok_rows:, :] = (weight - high.astype(F32)).astype(BF16)


def spread_kernel(capacity, flags_ref, arrived_ref, out_ref):
    arrived = unfold(arrived_ref[...], capacity)
    total = arrived.shape[0]
    columns = out_ref.shape[3]
    source = lax.broadcasted_iota(I32, (total, 1), 0)
    target = lax.broadcasted_iota(I32, (1, total), 1)
    pick = (source == target % columns * 4 + target // columns).astype(BF16)
    rows = matmul(arrived, pick, ((0,), (0,))).astype(BF16)
    rows = [rows[:, g * columns : (g + 1) * columns] for g in range(4)]
    split = out_ref.shape[1] // 2
    for c in range(2 * split):
        xh = c // split
        swap = flags_ref[c]
        out_ref[swap, c] = rows[xh]
        out_ref[1 - swap, c] = rows[2 + xh]


def mlp_kernel(rows_ref, up_ref, down_ref, out_ref):
    width, hidden_width = down_ref.shape
    columns = rows_ref.shape[2]
    projected = matmul(up_ref[...], jnp.concatenate([rows_ref[0], rows_ref[1]], axis=1))
    gate = projected[:hidden_width]
    hidden = (gate / (1.0 + jnp.exp(-gate)) * projected[hidden_width:]).astype(BF16)
    step = width // 2
    for c in range(2):
        here = slice(c * step, (c + 1) * step)
        value = matmul(down_ref[here, :], hidden).astype(BF16)
        out_ref[0, here, :] = value[:, :columns]
        out_ref[1, here, :] = value[:, columns:]


def merge_kernel(flags_ref, returned_ref, out_ref):
    halves, slots, part, columns = returned_ref.shape
    split = slots // 2
    sums = []
    for group in range(4):
        home, xh = group // 2, group % 2
        total = jnp.zeros((part, columns), F32)
        for c in range(xh * split, (xh + 1) * split):
            source = home ^ flags_ref[c]
            total = total + returned_ref[source, c].astype(F32)
        sums.append(total.astype(BF16))
    target = lax.broadcasted_iota(I32, (4 * columns, 1), 0)
    held = lax.broadcasted_iota(I32, (1, 4 * columns), 1)
    put = (target == held % columns * 4 + held // columns).astype(BF16)
    out_ref[...] = fold(matmul(put, jnp.concatenate(sums, axis=1), ((1,), (1,))), out_ref.shape)


def combine_kernel(capacity, weight_ref, back_ref, mixed_ref):
    tok_rows = mixed_ref.shape[0]
    both = matmul(weight_ref[...], unfold(back_ref[...], capacity))
    mixed_ref[...] = both[:tok_rows] + both[tok_rows:]


def call(name, kernel, shape, dtype, specs, *args):
    return pl.pallas_call(
        kernel,
        out_shape=jax.ShapeDtypeStruct(shape, dtype),
        in_specs=specs,
        out_specs=VMEM,
        compiler_params=PARAMS,
        name=name,
    )(*args)


def swap(value, axes):
    return lax.all_to_all(value, axes, split_axis=0, concat_axis=0, tiled=True)


def per_device(tokens, gate_scores, routes, balanced, gate_up, down_proj):
    split = lax.axis_size("e")
    lines = lax.axis_size("z")
    slots = 2 * split
    tok_rows, top_count = routes.shape
    width = tokens.shape[1]
    part = width // slots
    expert_count = 4 * lines
    capacity = min(tok_rows, max(2, 2 * tok_rows * top_count // expert_count))
    columns = lines * capacity
    folded = (lines, 4, capacity * part)
    xh, e, z = (lax.axis_index(n) for n in ("xh", "e", "z"))

    mine = lax.dynamic_slice_in_dim(tokens, (xh * split + e) * part, part, 1)
    outgoing = call(
        "dispatch",
        lambda *refs: dispatch_kernel(lines, capacity, *refs),
        folded,
        BF16,
        [VMEM, VMEM],
        routes.T,
        mine,
    )
    arrived = swap(outgoing, "z")

    own_flag = lax.dynamic_index_in_dim(balanced[:, 0], z, 0, keepdims=True)
    flags = lax.all_gather(own_flag, ("xh", "e"), axis=0, tiled=True)
    weight = call(
        "weight",
        lambda *refs: weight_kernel(lines, capacity, *refs),
        (2 * tok_rows, 4 * columns),
        BF16,
        [VMEM, VMEM],
        routes,
        gate_scores,
    )
    up, down = gate_up[0, 0].T, down_proj[0, 0].T
    arrived, up, down, weight = lax.optimization_barrier((arrived, up, down, weight))

    spread = call(
        "spread",
        lambda *refs: spread_kernel(capacity, *refs),
        (2, slots, part, columns),
        BF16,
        [SMEM, VMEM],
        flags,
        arrived,
    )
    gathered = swap(spread.reshape(2 * slots, part, columns), PLANE)
    partial_value = call(
        "tile_mlp",
        mlp_kernel,
        (2, width, columns),
        BF16,
        [VMEM, VMEM, VMEM],
        gathered.reshape(2, width, columns),
        up,
        down,
    )
    returned = swap(partial_value.reshape(2 * slots, part, columns), PLANE)
    merged = call(
        "merge",
        merge_kernel,
        folded,
        BF16,
        [SMEM, VMEM],
        flags,
        returned.reshape(2, slots, part, columns),
    )
    back = swap(merged, "z")
    return call(
        "combine",
        lambda *refs: combine_kernel(capacity, *refs),
        (tok_rows, part),
        F32,
        [VMEM, VMEM],
        weight,
        back,
    )


def solution(mesh):
    ep, dp = mesh.shape["ep"], mesh.shape["dp"]
    fine = Mesh(mesh.devices.reshape(2, ep // 2, 2, dp // 2), AXES)
    tok, exp = ("yh", "z"), ("xh", "e")
    placed = (
        P(tok, None),
        P(tok, None),
        P(tok, None),
        P(None, exp),
        P(tok, exp, None, None),
        P(tok, exp, None, None),
    )
    return jax.shard_map(
        per_device, mesh=fine, in_specs=placed, out_specs=P(tok, exp), check_vma=False
    )
```

```python
import jax
import jax.numpy as jnp
from jax import lax
from jax.experimental import pallas as pl
from jax.experimental.pallas import tpu as pltpu
from jax.sharding import Mesh, PartitionSpec as P

ROUTE_SCALE = 2.5
AXES = ("xh", "e", "yh", "z")
PLANE = ("yh", "xh", "e")
BF16, F32, I32 = jnp.bfloat16, jnp.float32, jnp.int32
SMEM = pl.BlockSpec(memory_space=pltpu.SMEM)
VMEM = pl.BlockSpec(memory_space=pltpu.VMEM)
PARAMS = pltpu.CompilerParams(vmem_limit_bytes=24 * 2**20)


def matmul(a, b, dims=((1,), (0,))):
    return lax.dot_general(a, b, (dims, ((), ())), preferred_element_type=F32)


def earlier(count):
    return (
        lax.broadcasted_iota(I32, (count, count), 0) > lax.broadcasted_iota(I32, (count, count), 1)
    ).astype(BF16)


def column_of(lines, capacity, shape):
    column = lax.broadcasted_iota(I32, shape, 1)
    place = column // (4 * lines)
    line = (column // 4 + lines // 2) % lines
    group = column % 4
    return (group // 2 * lines + line) * 2 + group % 2, place


def fold(value, shape):
    places = shape[2] // value.shape[1]
    rows = value.shape[0] // places
    wide = [value[p * rows : (p + 1) * rows] for p in range(places)]
    return jnp.concatenate(wide, axis=1).reshape(shape).astype(BF16)


def unfold(value, places):
    lines, groups, width = value.shape
    flat = value.reshape(lines * groups, width)
    part = width // places
    return jnp.concatenate([flat[:, p * part : (p + 1) * part] for p in range(places)], axis=0)


def dispatch_kernel(lines, capacity, routes_ref, mine_ref, out_ref):
    top_count, tok_rows = routes_ref.shape
    rows = lines * 4 * capacity
    expert_at, place = column_of(lines, capacity, (1, rows))
    unit = (
        lax.broadcasted_iota(I32, (top_count, top_count), 0)
        == lax.broadcasted_iota(I32, (top_count, top_count), 1)
    ).astype(BF16)
    routes = matmul(routes_ref[...].astype(F32).astype(BF16), unit, ((0,), (0,)))
    member = jnp.zeros((tok_rows, rows), F32)
    for k in range(top_count):
        member = jnp.where(routes[:, k : k + 1] == expert_at.astype(F32), 1.0, member)
    rank = matmul(earlier(tok_rows), member.astype(BF16))
    chosen = jnp.where(rank == place.astype(F32), member, 0.0).astype(BF16)
    out_ref[...] = fold(matmul(chosen, mine_ref[...], ((0,), (0,))), out_ref.shape)


def weight_kernel(lines, capacity, routes_ref, scores_ref, weight_ref):
    tok_rows, top_count = routes_ref.shape
    rows = lines * 4 * capacity
    expert_at, place = column_of(lines, capacity, (1, rows))
    routes = routes_ref[...]
    scores = scores_ref[...]
    scaled = scores / jnp.sum(scores, axis=1, keepdims=True) * ROUTE_SCALE
    weight = jnp.zeros((tok_rows, rows), F32)
    member = jnp.zeros((tok_rows, rows), F32)
    for k in range(top_count):
        match = routes[:, k : k + 1] == expert_at
        member = jnp.where(match, 1.0, member)
        weight = jnp.where(match, scaled[:, k : k + 1], weight)
    rank = matmul(earlier(tok_rows), member.astype(BF16))
    weight = jnp.where(rank == place.astype(F32), weight, 0.0)
    high = weight.astype(BF16)
    weight_ref[:tok_rows, :] = high
    weight_ref[tok_rows:, :] = (weight - high.astype(F32)).astype(BF16)


def spread_kernel(capacity, flags_ref, arrived_ref, out_ref):
    arrived = unfold(arrived_ref[...], capacity)
    total = arrived.shape[0]
    columns = out_ref.shape[3]
    source = lax.broadcasted_iota(I32, (total, 1), 0)
    target = lax.broadcasted_iota(I32, (1, total), 1)
    pick = (source == target % columns * 4 + target // columns).astype(BF16)
    rows = matmul(arrived, pick, ((0,), (0,))).astype(BF16)
    rows = [rows[:, g * columns : (g + 1) * columns] for g in range(4)]
    split = out_ref.shape[1] // 2
    for c in range(2 * split):
        xh = c // split
        swap = flags_ref[c]
        out_ref[swap, c] = rows[xh]
        out_ref[1 - swap, c] = rows[2 + xh]


def mlp_kernel(rows_ref, up_ref, down_ref, out_ref):
    width, hidden_width = down_ref.shape
    columns = rows_ref.shape[2]
    projected = matmul(up_ref[...], jnp.concatenate([rows_ref[0], rows_ref[1]], axis=1))
    gate = projected[:hidden_width]
    hidden = (gate / (1.0 + jnp.exp(-gate)) * projected[hidden_width:]).astype(BF16)
    step = width // 2
    for c in range(2):
        here = slice(c * step, (c + 1) * step)
        value = matmul(down_ref[here, :], hidden).astype(BF16)
        out_ref[0, here, :] = value[:, :columns]
        out_ref[1, here, :] = value[:, columns:]


def merge_kernel(flags_ref, returned_ref, out_ref):
    halves, slots, part, columns = returned_ref.shape
    split = slots // 2
    sums = []
    for group in range(4):
        home, xh = group // 2, group % 2
        total = jnp.zeros((part, columns), F32)
        for c in range(xh * split, (xh + 1) * split):
            source = home ^ flags_ref[c]
            total = total + returned_ref[source, c].astype(F32)
        sums.append(total.astype(BF16))
    target = lax.broadcasted_iota(I32, (4 * columns, 1), 0)
    held = lax.broadcasted_iota(I32, (1, 4 * columns), 1)
    put = (target == held % columns * 4 + held // columns).astype(BF16)
    out_ref[...] = fold(matmul(put, jnp.concatenate(sums, axis=1), ((1,), (1,))), out_ref.shape)


def combine_kernel(capacity, weight_ref, back_ref, mixed_ref):
    tok_rows = mixed_ref.shape[0]
    both = matmul(weight_ref[...], unfold(back_ref[...], capacity))
    mixed_ref[...] = both[:tok_rows] + both[tok_rows:]


def call(name, kernel, shape, dtype, specs, *args):
    return pl.pallas_call(
        kernel,
        out_shape=jax.ShapeDtypeStruct(shape, dtype),
        in_specs=specs,
        out_specs=VMEM,
        compiler_params=PARAMS,
        name=name,
    )(*args)


def swap(value, axes):
    order = None
    if axes == "z":
        lines = lax.axis_size("z")
        order = [[(z + lines // 2) % lines for z in range(lines)]]
    return lax.all_to_all(
        value, axes, split_axis=0, concat_axis=0, axis_index_groups=order, tiled=True
    )


def per_device(tokens, gate_scores, routes, balanced, gate_up, down_proj):
    split = lax.axis_size("e")
    lines = lax.axis_size("z")
    slots = 2 * split
    tok_rows, top_count = routes.shape
    width = tokens.shape[1]
    part = width // slots
    expert_count = 4 * lines
    capacity = min(tok_rows, max(2, 2 * tok_rows * top_count // expert_count))
    columns = lines * capacity
    folded = (lines, 4, capacity * part)
    xh, e, z = (lax.axis_index(n) for n in ("xh", "e", "z"))

    mine = lax.dynamic_slice_in_dim(tokens, (xh * split + e) * part, part, 1)
    outgoing = call(
        "dispatch",
        lambda *refs: dispatch_kernel(lines, capacity, *refs),
        folded,
        BF16,
        [VMEM, VMEM],
        routes.T,
        mine,
    )
    arrived = swap(outgoing, "z")

    own_flag = lax.dynamic_index_in_dim(balanced[:, 0], z, 0, keepdims=True)
    flags = lax.all_gather(own_flag, ("xh", "e"), axis=0, tiled=True)
    weight = call(
        "weight",
        lambda *refs: weight_kernel(lines, capacity, *refs),
        (2 * tok_rows, 4 * columns),
        BF16,
        [VMEM, VMEM],
        routes,
        gate_scores,
    )
    up, down = gate_up[0, 0].T, down_proj[0, 0].T
    arrived, up, down, weight = lax.optimization_barrier((arrived, up, down, weight))

    spread = call(
        "spread",
        lambda *refs: spread_kernel(capacity, *refs),
        (2, slots, part, columns),
        BF16,
        [SMEM, VMEM],
        flags,
        arrived,
    )
    gathered = swap(spread.reshape(2 * slots, part, columns), PLANE)
    partial_value = call(
        "tile_mlp",
        mlp_kernel,
        (2, width, columns),
        BF16,
        [VMEM, VMEM, VMEM],
        gathered.reshape(2, width, columns),
        up,
        down,
    )
    returned = swap(partial_value.reshape(2 * slots, part, columns), PLANE)
    merged = call(
        "merge",
        merge_kernel,
        folded,
        BF16,
        [SMEM, VMEM],
        flags,
        returned.reshape(2, slots, part, columns),
    )
    back = swap(merged, "z")
    return call(
        "combine",
        lambda *refs: combine_kernel(capacity, *refs),
        (tok_rows, part),
        F32,
        [VMEM, VMEM],
        weight,
        back,
    )


def solution(mesh):
    ep, dp = mesh.shape["ep"], mesh.shape["dp"]
    fine = Mesh(mesh.devices.reshape(2, ep // 2, 2, dp // 2), AXES)
    tok, exp = ("yh", "z"), ("xh", "e")
    placed = (
        P(tok, None),
        P(tok, None),
        P(tok, None),
        P(None, exp),
        P(tok, exp, None, None),
        P(tok, exp, None, None),
    )
    return jax.shard_map(
        per_device, mesh=fine, in_specs=placed, out_specs=P(tok, exp), check_vma=False
    )
```

```python
import jax
import jax.numpy as jnp
from jax import lax
from jax.experimental import pallas as pl
from jax.experimental.pallas import tpu as pltpu
from jax.sharding import Mesh, PartitionSpec as P

ROUTE_SCALE = 2.5
AXES = ("xh", "e", "yh", "z")
PLANE = ("yh", "xh", "e")
BF16, F32, I32 = jnp.bfloat16, jnp.float32, jnp.int32
SMEM = pl.BlockSpec(memory_space=pltpu.SMEM)
VMEM = pl.BlockSpec(memory_space=pltpu.VMEM)
HBM = pl.BlockSpec(memory_space=pltpu.HBM)


def matmul(a, b, dims=((1,), (0,))):
    return lax.dot_general(a, b, (dims, ((), ())), preferred_element_type=F32)


def earlier(count):
    return (
        lax.broadcasted_iota(I32, (count, count), 0) > lax.broadcasted_iota(I32, (count, count), 1)
    ).astype(BF16)


def column_of(lines, capacity, shape):
    column = lax.broadcasted_iota(I32, shape, 1)
    place = column // (4 * lines)
    line = (column // 4 + lines // 2) % lines
    group = column % 4
    return (group // 2 * lines + line) * 2 + group % 2, place


def fold(value, shape):
    places = shape[2] // value.shape[1]
    rows = value.shape[0] // places
    wide = [value[p * rows : (p + 1) * rows] for p in range(places)]
    return jnp.concatenate(wide, axis=1).reshape(shape).astype(BF16)


def unfold(value, places):
    lines, groups, width = value.shape
    flat = value.reshape(lines * groups, width)
    part = width // places
    return jnp.concatenate([flat[:, p * part : (p + 1) * part] for p in range(places)], axis=0)


def dispatch_kernel(
    lines, capacity, part, start_ref, routes_hbm, tokens_hbm, out_ref, routes_ref, window_ref, sems
):
    window = window_ref.shape[1]
    base = jnp.minimum(start_ref[0] // 128 * 128, tokens_hbm.shape[1] - window)
    here = pl.ds(pl.multiple_of(base, 128), window)
    fetch_routes = pltpu.make_async_copy(routes_hbm, routes_ref, sems.at[0])
    fetch_tokens = pltpu.make_async_copy(tokens_hbm.at[:, here], window_ref, sems.at[1])
    fetch_routes.start()
    fetch_tokens.start()
    fetch_routes.wait()
    top_count, tok_rows = routes_ref.shape
    rows = lines * 4 * capacity
    expert_at, place = column_of(lines, capacity, (1, rows))
    unit = (
        lax.broadcasted_iota(I32, (top_count, top_count), 0)
        == lax.broadcasted_iota(I32, (top_count, top_count), 1)
    ).astype(BF16)
    routes = matmul(routes_ref[...].astype(F32).astype(BF16), unit, ((0,), (0,)))
    member = jnp.zeros((tok_rows, rows), F32)
    for k in range(top_count):
        member = jnp.where(routes[:, k : k + 1] == expert_at.astype(F32), 1.0, member)
    rank = matmul(earlier(tok_rows), member.astype(BF16))
    chosen = jnp.where(rank == place.astype(F32), member, 0.0).astype(BF16)
    fetch_tokens.wait()
    shift = lax.rem(window - (start_ref[0] - base), window)
    mine = pltpu.roll(window_ref[...].astype(F32), shift, 1)[:, :part].astype(BF16)
    out_ref[...] = fold(matmul(chosen, mine, ((0,), (0,))), out_ref.shape)


def weight_kernel(lines, capacity, routes_ref, scores_ref, weight_ref):
    tok_rows, top_count = routes_ref.shape
    rows = lines * 4 * capacity
    expert_at, place = column_of(lines, capacity, (1, rows))
    routes = routes_ref[...]
    scores = scores_ref[...]
    scaled = scores / jnp.sum(scores, axis=1, keepdims=True) * ROUTE_SCALE
    weight = jnp.zeros((tok_rows, rows), F32)
    member = jnp.zeros((tok_rows, rows), F32)
    for k in range(top_count):
        match = routes[:, k : k + 1] == expert_at
        member = jnp.where(match, 1.0, member)
        weight = jnp.where(match, scaled[:, k : k + 1], weight)
    rank = matmul(earlier(tok_rows), member.astype(BF16))
    weight = jnp.where(rank == place.astype(F32), weight, 0.0)
    high = weight.astype(BF16)
    weight_ref[:tok_rows, :] = high
    weight_ref[tok_rows:, :] = (weight - high.astype(F32)).astype(BF16)


def spread_kernel(capacity, flags_ref, arrived_ref, out_ref):
    arrived = unfold(arrived_ref[...], capacity)
    total = arrived.shape[0]
    columns = out_ref.shape[3]
    source = lax.broadcasted_iota(I32, (total, 1), 0)
    target = lax.broadcasted_iota(I32, (1, total), 1)
    pick = (source == target % columns * 4 + target // columns).astype(BF16)
    rows = matmul(arrived, pick, ((0,), (0,))).astype(BF16)
    rows = [rows[:, g * columns : (g + 1) * columns] for g in range(4)]
    split = out_ref.shape[1] // 2
    for c in range(2 * split):
        xh = c // split
        swap = flags_ref[c]
        out_ref[swap, c] = rows[xh]
        out_ref[1 - swap, c] = rows[2 + xh]


def mlp_kernel(rows_ref, up_ref, down_ref, out_ref):
    width, hidden_width = down_ref.shape
    columns = rows_ref.shape[2]
    projected = matmul(up_ref[...], jnp.concatenate([rows_ref[0], rows_ref[1]], axis=1))
    gate = projected[:hidden_width]
    hidden = (gate / (1.0 + jnp.exp(-gate)) * projected[hidden_width:]).astype(BF16)
    step = width // 2
    for c in range(2):
        here = slice(c * step, (c + 1) * step)
        value = matmul(down_ref[here, :], hidden).astype(BF16)
        out_ref[0, here, :] = value[:, :columns]
        out_ref[1, here, :] = value[:, columns:]


def merge_kernel(flags_ref, returned_ref, out_ref):
    halves, slots, part, columns = returned_ref.shape
    split = slots // 2
    sums = []
    for group in range(4):
        home, xh = group // 2, group % 2
        total = jnp.zeros((part, columns), F32)
        for c in range(xh * split, (xh + 1) * split):
            source = home ^ flags_ref[c]
            total = total + returned_ref[source, c].astype(F32)
        sums.append(total.astype(BF16))
    target = lax.broadcasted_iota(I32, (4 * columns, 1), 0)
    held = lax.broadcasted_iota(I32, (1, 4 * columns), 1)
    put = (target == held % columns * 4 + held // columns).astype(BF16)
    out_ref[...] = fold(matmul(put, jnp.concatenate(sums, axis=1), ((1,), (1,))), out_ref.shape)


def combine_kernel(capacity, weight_ref, back_ref, mixed_ref):
    tok_rows = mixed_ref.shape[0]
    both = matmul(weight_ref[...], unfold(back_ref[...], capacity))
    mixed_ref[...] = both[:tok_rows] + both[tok_rows:]


def call(name, kernel, shape, dtype, specs, *args, scratch=(), limit=24):
    return pl.pallas_call(
        kernel,
        out_shape=jax.ShapeDtypeStruct(shape, dtype),
        in_specs=specs,
        out_specs=VMEM,
        scratch_shapes=scratch,
        compiler_params=pltpu.CompilerParams(vmem_limit_bytes=limit * 2**20),
        name=name,
    )(*args)


def swap(value, axes):
    order = None
    if axes == "z":
        lines = lax.axis_size("z")
        order = [[(z + lines // 2) % lines for z in range(lines)]]
    return lax.all_to_all(
        value, axes, split_axis=0, concat_axis=0, axis_index_groups=order, tiled=True
    )


def per_device(tokens, gate_scores, routes, balanced, gate_up, down_proj):
    split = lax.axis_size("e")
    lines = lax.axis_size("z")
    slots = 2 * split
    tok_rows, top_count = routes.shape
    width = tokens.shape[1]
    part = width // slots
    expert_count = 4 * lines
    capacity = min(tok_rows, max(2, 2 * tok_rows * top_count // expert_count))
    columns = lines * capacity
    folded = (lines, 4, capacity * part)
    xh, e, z = (lax.axis_index(n) for n in ("xh", "e", "z"))

    start = ((xh * split + e) * part).astype(I32).reshape(1)
    window = -(-(part + 127) // 128) * 128
    outgoing = call(
        "dispatch",
        lambda *refs: dispatch_kernel(lines, capacity, part, *refs),
        folded,
        BF16,
        [SMEM, HBM, HBM],
        start,
        routes.T,
        tokens,
        limit=63,
        scratch=[
            pltpu.VMEM((top_count, tok_rows), I32),
            pltpu.VMEM((tok_rows, window), BF16),
            pltpu.SemaphoreType.DMA((2,)),
        ],
    )
    arrived = swap(outgoing, "z")

    own_flag = lax.dynamic_index_in_dim(balanced[:, 0], z, 0, keepdims=True)
    flags = lax.all_gather(own_flag, ("xh", "e"), axis=0, tiled=True)
    weight = call(
        "weight",
        lambda *refs: weight_kernel(lines, capacity, *refs),
        (2 * tok_rows, 4 * columns),
        BF16,
        [VMEM, VMEM],
        routes,
        gate_scores,
    )
    up, down = gate_up[0, 0].T, down_proj[0, 0].T
    arrived, up, down, weight = lax.optimization_barrier((arrived, up, down, weight))

    spread = call(
        "spread",
        lambda *refs: spread_kernel(capacity, *refs),
        (2, slots, part, columns),
        BF16,
        [SMEM, VMEM],
        flags,
        arrived,
    )
    gathered = swap(spread.reshape(2 * slots, part, columns), PLANE)
    partial_value = call(
        "tile_mlp",
        mlp_kernel,
        (2, width, columns),
        BF16,
        [VMEM, VMEM, VMEM],
        gathered.reshape(2, width, columns),
        up,
        down,
    )
    returned = swap(partial_value.reshape(2 * slots, part, columns), PLANE)
    merged = call(
        "merge",
        merge_kernel,
        folded,
        BF16,
        [SMEM, VMEM],
        flags,
        returned.reshape(2, slots, part, columns),
    )
    back = swap(merged, "z")
    return call(
        "combine",
        lambda *refs: combine_kernel(capacity, *refs),
        (tok_rows, part),
        F32,
        [VMEM, VMEM],
        weight,
        back,
    )


def solution(mesh):
    ep, dp = mesh.shape["ep"], mesh.shape["dp"]
    fine = Mesh(mesh.devices.reshape(2, ep // 2, 2, dp // 2), AXES)
    tok, exp = ("yh", "z"), ("xh", "e")
    placed = (
        P(tok, None),
        P(tok, None),
        P(tok, None),
        P(None, exp),
        P(tok, exp, None, None),
        P(tok, exp, None, None),
    )
    return jax.shard_map(
        per_device, mesh=fine, in_specs=placed, out_specs=P(tok, exp), check_vma=False
    )
```
